128 devices in a mesh: wide: 16 (over y, x_hi, core), band: 8 (over z, x_lo).
Axes of the slice: x: 4 (x_hi: 2, x_lo: 2; x = x_hi * 2 + x_lo), y: 4, z: 4, core: 2. Of those that a mesh axis runs over, the one named last changes fastest.
Arguments:
- samples: bfloat16 [16, 512, 18432], P(None, 'band', 'wide'), may hold values from -12 to 12
- offsets: int32 [32], P('wide'), may hold values from 0 to 64
Outputs:
- correlations: bfloat16 [2, 512, 8192, 128], P(None, 'band', 'wide')
The draws below stay inside these ranges and needn't reach their ends.
All inputs are finite; a program needn't handle non-finite values.
Results may differ from the reference program's by a relative error of at most 0.0065.
Values may be sent and summed in bfloat16 or wider, within the bound.
A program may use at most 192 MiB of HBM per device.

```python
import math
import jax
import jax.numpy as jnp
from jax import lax

F = 256
MARGIN = 64
LAGS = 128
ROWS = 1024
NSUB = 32
TIME = 18432
GROUPS = 16
CBLK = 512


def draw_samples(key, part):
    key = jax.random.fold_in(key, 11)
    gain_key, noise_key = jax.random.split(key, 2)
    gains = jnp.exp(jax.random.uniform(gain_key, (GROUPS, CBLK, 1), jnp.float32, math.log(0.3), math.log(3.0)))
    values = jax.random.normal(noise_key, (GROUPS, CBLK, TIME), jnp.float32) * gains
    return jnp.clip(values, -12.0, 12.0).astype(jnp.bfloat16)


def set_ends(values, rng, low, top_value):
    longest = values.shape.index(max(values.shape))
    spots = []
    for shift in (0, 1):
        where = [jax.random.randint(jax.random.fold_in(rng, axis), (), 0, length) for axis, length in enumerate(values.shape)]
        where[longest] = (where[longest] + shift) % values.shape[longest]
        spots.append(tuple(where))
    return values.at[spots[0]].set(low).at[spots[1]].set(top_value)


def setup_inputs(seed: int = 0) -> dict:
    key_list = jax.random.split(jax.random.key(seed), 3)
    return {
        "samples": draw_samples(jax.random.fold_in(key_list[2], 71), 0),
        "offsets": set_ends(jax.random.randint(key_list[1], (NSUB,), 0, MARGIN + 1), jax.random.fold_in(key_list[1], 1), 0, MARGIN).astype(jnp.int32),
    }


def dft_table(seg_len, bin_count):
    sample_index = jnp.arange(seg_len, dtype=jnp.int32)
    bin_index = jnp.arange(bin_count, dtype=jnp.int32)
    phase = bin_index[:, None] * sample_index[None, :] % seg_len
    angle = 2.0 * math.pi / seg_len * phase.astype(jnp.float32)
    window = 0.5 - 0.5 * jnp.cos(2.0 * math.pi / seg_len * (sample_index.astype(jnp.float32) + 0.5))
    return jnp.concatenate([jnp.cos(angle) * window[None, :], -jnp.sin(angle) * window[None, :]], 0).astype(jnp.bfloat16)

def lag_table(seg_len, bin_count, lag_count):
    bin_index = jnp.arange(bin_count, dtype=jnp.int32)
    shifts = jnp.arange(lag_count, dtype=jnp.int32) - lag_count // 2
    phase = bin_index[:, None] * shifts[None, :] % seg_len
    angle = 2.0 * math.pi / seg_len * phase.astype(jnp.float32)
    factor = 1.0 / math.sqrt(bin_count)
    return jnp.concatenate([jnp.cos(angle) * factor, -jnp.sin(angle) * factor], 0).astype(jnp.bfloat16)

def whiten(spectrum, bin_count):
    real_part = spectrum[..., :bin_count]
    imag_part = spectrum[..., bin_count:]
    spectral_power = real_part * real_part + imag_part * imag_part
    level_mean = lax.optimization_barrier(jnp.mean(spectral_power, axis=-1, keepdims=True))
    divisor = jnp.sqrt(spectral_power + 0.25 * level_mean + 1e-06)
    return spectrum / jnp.concatenate([divisor, divisor], -1)

def reference(samples, offsets):
    groups, cblk, total = samples.shape
    channels = groups * cblk
    nsub = offsets.shape[0]
    span = total // nsub
    seg_len = 2 * F
    table = dft_table(seg_len, F)
    lagtab = lag_table(seg_len, F, LAGS)
    flattened = samples.reshape(channels, total)

    def sub_spectrum(sub_index):
        start = (sub_index * span + offsets[sub_index]).astype(jnp.int32)
        window = lax.dynamic_slice_in_dim(flattened, start, seg_len, 1)
        spectrum = jnp.dot(window, table.T, preferred_element_type=jnp.float32)
        return whiten(spectrum, F).astype(jnp.bfloat16)
    spectra = lax.map(sub_spectrum, jnp.arange(nsub, dtype=jnp.int32))
    columns = spectra.astype(jnp.float32).reshape(nsub, channels, 2, F)
    block_rows = 16
    factor = 1.0 / math.sqrt(nsub)

    def block_corr(block_index):
        start = (block_index * block_rows).astype(jnp.int32)
        row_block = lax.dynamic_slice_in_dim(columns, start, block_rows, 1)
        turned = jnp.stack([row_block[:, :, 1], -row_block[:, :, 0]], 2)
        real_part = jnp.einsum('krpf,kcpf->rcf', row_block, columns)
        imag_part = jnp.einsum('krpf,kcpf->rcf', turned, columns)
        row_channel = start + jnp.arange(block_rows, dtype=jnp.int32)
        column_index = jnp.arange(channels, dtype=jnp.int32)
        weights = jnp.where(row_channel[:, None] == column_index[None, :], 0.0, factor).astype(jnp.float32)
        stacked = (jnp.stack([real_part, imag_part], 2) * weights[:, :, None, None]).astype(jnp.bfloat16)
        corr = jnp.dot(stacked.reshape(block_rows * channels, 2 * F), lagtab, preferred_element_type=jnp.float32)
        return corr.astype(jnp.bfloat16).reshape(block_rows, channels, LAGS)
    result = lax.map(block_corr, jnp.arange(ROWS // block_rows, dtype=jnp.int32))
    return result.reshape(ROWS // cblk, cblk, channels, LAGS)
```

```python
import math

import jax
import jax.numpy as jnp
import ml_dtypes
import numpy as np
from jax import lax
from jax.experimental import pallas as pl
from jax.experimental.pallas import tpu as pltpu
from jax.sharding import PartitionSpec as P

MESH = pl.DeviceIdType.MESH
NQ = 4
NJ = 8
PW = 24
FAC = 1 / math.sqrt(32)


def dft_np():
    n=np.arange(512); f=np.arange(256)
    ph=(f[:,None]*n[None,:])%512
    ang=2*np.pi/512*ph
    win=0.5-0.5*np.cos(2*np.pi/512*(n+0.5))
    t=np.concatenate([np.cos(ang)*win, -np.sin(ang)*win],0).astype(ml_dtypes.bfloat16)
    t=t.reshape(2,32,8,512).transpose(1,0,2,3).reshape(512,512).astype(np.float32)
    return np.concatenate([t,np.zeros((512,128),np.float32)],1)

def lag_np():
    f=np.arange(256); l=np.arange(128)-64
    ph=(f[:,None]*l[None,:])%512
    ang=2*np.pi/512*ph
    t=np.concatenate([np.cos(ang)/16,-np.sin(ang)/16],0).astype(ml_dtypes.bfloat16)
    return t.reshape(2,256,128).transpose(2,1,0).reshape(128,512).copy()

def spec_kernel(off_ref, tab_ref, s_ref, x_ref, tk):
    i=pl.program_id(0)
    @pl.when(i==0)
    def _():
        for k in range(2):
            t=pltpu.roll(tab_ref[...], off_ref[k]+64*k, 1)
            tk[k]=t.astype(jnp.bfloat16)
    s=s_ref[...].reshape(128,1152)
    a0=lax.dot_general(tk[0], s[:, :640], (((1,),(1,)),((),())), preferred_element_type=jnp.float32)
    a1=lax.dot_general(tk[1], s[:, 512:], (((1,),(1,)),((),())), preferred_element_type=jnp.float32)
    lane=lax.broadcasted_iota(jnp.int32,(512,128),1)<64
    g0=jnp.where(lane,a0,pltpu.roll(a1,64,1))
    g1=jnp.where(lane,pltpu.roll(a0,64,1),a1)
    for j,g in enumerate((g0,g1)):
        v=g.reshape(32,2,8,128)
        re=v[:,0]; im=v[:,1]
        pw=re*re+im*im
        level=jnp.sum(jnp.sum(pw,0),0,keepdims=True)*(0.25/256.0)+1e-6
        inv=lax.rsqrt(pw+level[None])
        x_ref[j]=jnp.stack([re*inv,im*inv],1).reshape(32,16,128).astype(jnp.bfloat16)

def spectra(samples, offsets):
    return pl.pallas_call(spec_kernel,
      grid=(8,),
      in_specs=[pl.BlockSpec(memory_space=pltpu.SMEM), pl.BlockSpec((512,640),lambda i:(0,0)), pl.BlockSpec((2,64,1152),lambda i:(i,0,0))],
      out_specs=pl.BlockSpec((2,32,16,128),lambda i:(i,0,0,0)),
      out_shape=jax.ShapeDtypeStruct((16,32,16,128),jnp.bfloat16),
      scratch_shapes=[pltpu.VMEM((2,512,640),jnp.bfloat16)],
      compiler_params=pltpu.CompilerParams(vmem_limit_bytes=32*2**20),
    )(offsets, jnp.asarray(dft_np()), samples)

def relayout_quarter(rcv, tmp, hold, q):
    @pl.loop(0, 8)
    def _(fi):
        fg=q*8+fi
        for xs in range(2):
            for w in range(8):
                tmp[xs, w*PW:w*PW+16, :]=rcv[xs, w, fg].astype(jnp.float32)
        for xs in range(2):
            for f8 in range(8):
                re=tmp[xs, pl.ds(f8,8,stride=PW),:]
                im=tmp[xs, pl.ds(8+f8,8,stride=PW),:]
                hold[xs, fg*8+f8]=jnp.concatenate([re,im],0).astype(jnp.bfloat16)

def comm_kernel(x_ref, g2_ref, r_ref, rcv, tmp, hold,
                a_send, a_recv, r_send, r_recv, x_send, zp_send, zm_send, g_recv, l_sem):
    wide=lax.axis_index("wide"); band=lax.axis_index("band")
    y=wide//4; xhi=(wide//2)%2; core=wide%2
    z=band//2; xl=band%2
    zp=(z+1)%4; zm=(z+3)%4; z2=(z+2)%4
    def wid(y_,xh_,c_): return (y_*2+xh_)*2+c_
    def a2a_dev(t):
        dy=t//4; dx=(t//2)%2; dc=t%2
        y_=(y+dy)%4; xh_=(xhi+dx)%2; c_=(core+dc)%2
        return y_,xh_,c_,dx
    dev_x=(wide, z*2+(1-xl)); dev_zp=(wide, zp*2+xl); dev_zm=(wide, zm*2+xl)
    dev_xhi=(wid(y,1-xhi,core), band)
    dev_core=(wid(y,xhi,1-core), band)
    bar=pltpu.get_barrier_semaphore()
    @pl.loop(1,16)
    def _(t):
        y_,xh_,c_,dx=a2a_dev(t)
        pl.semaphore_signal(bar,1,device_id=(wid(y_,xh_,c_), z*2+(xl+dx)%2),device_id_type=MESH)
    for d in (dev_x,dev_zp,dev_zm,dev_xhi):
        pl.semaphore_signal(bar,1,device_id=d,device_id_type=MESH)
    pl.semaphore_wait(bar,19)

    def rc(src,dst,ss,rs,dev):
        return pltpu.make_async_remote_copy(src_ref=src,dst_ref=dst,send_sem=ss,recv_sem=rs,device_id=dev,device_id_type=MESH)

    row_src=x_ref.at[pl.ds(0,2)]
    rows_xhi=rc(row_src, r_ref.at[wide], r_send.at[0], r_recv.at[wide], dev_xhi)
    rows_xhi.start()
    row_local=pltpu.make_async_copy(row_src, r_ref.at[wide], l_sem.at[0])
    row_local.start()
    own_local=pltpu.make_async_copy(x_ref.at[wide], rcv.at[xhi, y*2+core], l_sem.at[1])
    own_local.start()
    def a2a_copy(t,q):
        y_,xh_,c_,dx=a2a_dev(t)
        fs=pl.ds(q*8,8)
        return rc(x_ref.at[wid(y_,xh_,c_),fs], rcv.at[xhi,y*2+core,fs], a_send.at[t,q], a_recv.at[wide,q],
                  (wid(y_,xh_,c_), z*2+(xl+dx)%2))
    def a2a_wait(t,q):
        dy=t//4; dx=(t//2)%2; dc=t%2
        y_=(y+4-dy)%4; xh_=(xhi+dx)%2; c_=(core+dc)%2
        fs=pl.ds(q*8,8)
        s=wid(y_,xh_,c_)
        rc(x_ref.at[s,fs], rcv.at[xh_,y_*2+c_,fs], a_send.at[t,q], a_recv.at[s,q], dev_x).wait_recv()
    for q in range(NQ):
        @pl.loop(1,16)
        def _(t):
            a2a_copy(t,q).start()
    def row_y(dy,s,slot):
        return rc(r_ref.at[s], r_ref.at[s], r_send.at[slot], r_recv.at[s], (wid((y+dy)%4,xhi,core),band))
    def row_y_own(dy):
        return rc(row_src, r_ref.at[wide], r_send.at[dy], r_recv.at[wide], (wid((y+dy)%4,xhi,core),band))
    for dy in (1,2,3):
        row_y_own(dy).start()
    own_core=rc(row_src, r_ref.at[wide], r_send.at[4], r_recv.at[wide], dev_core)
    own_core.start()

    def slot(zz,xx,cls): return zz*2+(xx+cls)%2, (xhi+cls)%2
    def unit(b,xs,j): return g2_ref.at[b,xs,pl.ds(j*32,32)]
    def send(src,b,xs,j,sems,dev):
        return rc(src, unit(b,xs,j), sems.at[b,xs,j], g_recv.at[b,xs,j], dev)
    def wait_unit(zz,xx,cls,j):
        b,xs=slot(zz,xx,cls)
        send(unit(b,xs,j),b,xs,j,x_send,dev_x).wait_recv()
        return b,xs
    own_local.wait()
    for q in range(NQ):
        @pl.loop(1,16)
        def _(t):
            a2a_wait(t,q)
        relayout_quarter(rcv,tmp,hold,q)
        @pl.loop(q*2,q*2+2)
        def _(j):
            for cls in range(2):
                b,xs=slot(z,xl,cls)
                src=hold.at[xs,pl.ds(j*32,32)]
                send(src,b,xs,j,x_send,dev_x).start()
                send(src,b,xs,j,zp_send,dev_zp).start()
                send(src,b,xs,j,zm_send,dev_zm).start()
                pltpu.make_async_copy(src,unit(b,xs,j),l_sem.at[2+cls*8+j]).start()
    ps=wid(y,1-xhi,core)
    rc(row_src,r_ref.at[ps],r_send.at[0],r_recv.at[ps],dev_x).wait_recv()
    for dy in (1,2,3):
        row_y(dy,ps,4+dy).start()
    rc(r_ref.at[ps],r_ref.at[ps],r_send.at[8],r_recv.at[ps],dev_core).start()
    def pass_core(dy,xh_,slot_):
        s=wid((y+dy)%4,xh_,core)
        rc(row_src,r_ref.at[s],r_send.at[0],r_recv.at[s],dev_x).wait_recv()
        rc(r_ref.at[s],r_ref.at[s],r_send.at[slot_],r_recv.at[s],dev_core).start()
    for dy in (1,3,2):
        pass_core(dy,xhi,8+dy)
    for dy in (1,3,2):
        pass_core(dy,1-xhi,11+dy)

    def fwd(b,xs,j):
        pass
    @pl.loop(0,NJ)
    def _(j):
        b,xs=wait_unit(z,1-xl,0,j)
        send(unit(b,xs,j),b,xs,j,zp_send,dev_zp).start()
        send(unit(b,xs,j),b,xs,j,zm_send,dev_zm).start()
        @pl.when(j==7)
        def _():
            b1,xs1=wait_unit(z,1-xl,1,j)
            send(unit(b1,xs1,j),b1,xs1,j,zp_send,dev_zp).start()
            send(unit(b1,xs1,j),b1,xs1,j,zm_send,dev_zm).start()
        for zz,parity,sems,dev in ((zm,0,zp_send,dev_zp),(zp,1,zm_send,dev_zm)):
            for cls in range(2):
                b,xs=wait_unit(zz,xl,cls,j)
                @pl.when(j%2==parity)
                def _():
                    send(unit(b,xs,j),b,xs,j,sems,dev).start()
                if cls==1:
                    @pl.when(j<7)
                    def _():
                        send(unit(b,xs,j),b,xs,j,x_send,dev_x).start()
    @pl.loop(0,NJ)
    def _(j):
        for zz,parity,sems,dev in ((zm,0,zp_send,dev_zp),(zp,1,zm_send,dev_zm)):
            b,xs=wait_unit(zz,1-xl,0,j)
            @pl.when(j%2==parity)
            def _():
                send(unit(b,xs,j),b,xs,j,sems,dev).start()
            @pl.when(j==7)
            def _():
                b1,xs1=wait_unit(zz,1-xl,1,j)
                if parity==1:
                    send(unit(b1,xs1,j),b1,xs1,j,sems,dev).start()
        wait_unit(z2,xl,0,j)
        b2,xs2=wait_unit(z2,xl,1,j)
        @pl.when(j<7)
        def _():
            send(unit(b2,xs2,j),b2,xs2,j,x_send,dev_x).start()
    @pl.loop(0,NJ)
    def _(j):
        wait_unit(z2,1-xl,0,j)
        @pl.when(j==7)
        def _():
            wait_unit(z2,1-xl,1,j)
        @pl.when(j<7)
        def _():
            for zz in (z,zm,zp,z2):
                wait_unit(zz,1-xl,1,j)
    for dy in range(4):
        for xh_ in range(2):
            s=wid((y+dy)%4,xh_,1-core)
            rc(row_src,r_ref.at[s],r_send.at[0],r_recv.at[s],dev_x).wait_recv()
    row_local.wait()
    for i in range(15):
        rc(row_src,r_ref.at[wide],r_send.at[i],r_recv.at[wide],dev_x).wait_send()
    @pl.loop(1,16)
    def _(t):
        for q in range(NQ):
            a2a_copy(t,q).wait_send()
    def ws(zz,xx,cls,j,sems):
        b,xs=slot(zz,xx,cls)
        send(unit(b,xs,j),b,xs,j,sems,dev_x).wait_send()
    @pl.loop(0,NJ)
    def _(j):
        for cls in range(2):
            b,xs=slot(z,xl,cls)
            pltpu.make_async_copy(hold.at[xs,pl.ds(j*32,32)],unit(b,xs,j),l_sem.at[2+cls*8+j]).wait()
            ws(z,xl,cls,j,x_send)
            ws(z,xl,cls,j,zp_send); ws(z,xl,cls,j,zm_send)
        ws(z,1-xl,0,j,zp_send); ws(z,1-xl,0,j,zm_send)
        @pl.when(j==7)
        def _():
            ws(z,1-xl,1,j,zp_send); ws(z,1-xl,1,j,zm_send)
        @pl.when(j<7)
        def _():
            for zz in (zm,zp,z2): ws(zz,xl,1,j,x_send)
        for zz,parity,sems in ((zm,0,zp_send),(zp,1,zm_send)):
            @pl.when(j%2==parity)
            def _():
                ws(zz,xl,0,j,sems); ws(zz,xl,1,j,sems); ws(zz,1-xl,0,j,sems)
            if parity==1:
                @pl.when(j==7)
                def _(): ws(zz,1-xl,1,j,sems)

def comm(x):
    D=pltpu.SemaphoreType.DMA
    return pl.pallas_call(comm_kernel,
      in_specs=[pl.BlockSpec(memory_space=pl.ANY)],
      out_specs=[pl.BlockSpec(memory_space=pl.ANY)]*2,
      out_shape=[jax.ShapeDtypeStruct((8,2,256,16,128),jnp.bfloat16), jax.ShapeDtypeStruct((16,2,32,16,128),jnp.bfloat16)],
      scratch_shapes=[pltpu.VMEM((2,8,32,16,128),jnp.bfloat16), pltpu.VMEM((2,8*PW,128),jnp.float32), pltpu.VMEM((2,256,16,128),jnp.bfloat16),
        D((16,4)),D((16,4)),D((16,)),D((16,)),D((8,2,8)),D((8,2,8)),D((8,2,8)),D((8,2,8)),D((18,))],
      compiler_params=pltpu.CompilerParams(collective_id=0,has_side_effects=True,vmem_limit_bytes=60*2**20),
    )(x)


def join2(a,b):
    return jnp.concatenate([a[:,:64],b[:,:64]],1), jnp.concatenate([a[:,64:],b[:,64:]],1)

def rowsk(r_ref,o_ref,tmp,tt):
    for w in range(16):
        y,xs,c=w//4,(w//2)%2,w%2
        for g in range(2):
            tmp[g,xs,(y*2+c)*PW:(y*2+c)*PW+16,:]=r_ref[w,g,0].astype(jnp.float32)
    for fp in range(4):
        ks=[];ts=[]
        for f8 in (2*fp,2*fp+1):
            parts=[]
            for g in range(2):
                re=[tmp[g,xs,pl.ds(f8,8,stride=PW),:] for xs in range(2)]
                im=[tmp[g,xs,pl.ds(8+f8,8,stride=PW),:] for xs in range(2)]
                parts.append((jnp.concatenate([re[0],im[0],re[1],im[1]],0), jnp.concatenate([im[0],-re[0],im[1],-re[1]],0)))
            a0,a1=join2(parts[0][0],parts[1][0]); ks+= [a0,a1]
            a0,a1=join2(parts[0][1],parts[1][1]); ts+= [a0,a1]
        K=jnp.concatenate(ks,0); T=jnp.concatenate(ts,0)
        tt[pl.ds(0,128,stride=2),:]=K.T
        tt[pl.ds(1,128,stride=2),:]=T.T
        o_ref[fp]=tt[...].astype(jnp.bfloat16)
def rows(r):
    return pl.pallas_call(rowsk,grid=(32,),
      in_specs=[pl.BlockSpec((16,2,1,16,128),lambda i:(0,0,i,0,0))],
      out_specs=pl.BlockSpec((4,256,128),lambda i:(i,0,0)),
      out_shape=jax.ShapeDtypeStruct((128,256,128),jnp.bfloat16),
      scratch_shapes=[pltpu.VMEM((2,2,8*PW,128),jnp.float32),pltpu.VMEM((256,128),jnp.float32)])(r)

FB, RB, U1, U2 = 64, 32, 16, 8
NS1, NS2 = 256 // FB, 128 // RB


def corr_kernel(info_ref, lag_ref, rt_ref, g_ref, o_ref, scr):
    z = pl.program_id(0)
    t = pl.program_id(1)

    @pl.when(t < NS1)
    def _():
        zero = jnp.zeros((64, 128), jnp.bfloat16)

        @pl.loop(0, FB // 2 // U1)
        def _(i0):
            for i1 in range(U1):
                fp = i0 * U1 + i1
                parts = []
                for j in range(2):
                    a = g_ref[0, :, fp * 2 + j].reshape(32, 128)
                    b = g_ref[1, :, fp * 2 + j].reshape(32, 128)
                    c = jnp.concatenate(join2(a, b), 0)
                    parts.append(jnp.concatenate([c, zero] if j == 0 else [zero, c], 1))
                s = jnp.dot(rt_ref[t * (FB // 2) + fp], jnp.concatenate(parts, 0), preferred_element_type=jnp.float32)
                for j in range(2):
                    scr[t * FB + fp * 2 + j] = s[:, j * 128 : (j + 1) * 128].astype(jnp.bfloat16).reshape(128, 2, 128)

    @pl.when(t >= NS1)
    def _():
        blk = t - NS1
        lag = lag_ref[...]

        @pl.loop(0, RB // 2 // U2)
        def _(i0):
            for i1 in range(U2):
                i = i0 * U2 + i1
                rhs = jnp.concatenate([scr[:, blk * RB + i * 2 + j].reshape(512, 128) for j in range(2)], 1)
                o = jnp.dot(lag, rhs, preferred_element_type=jnp.float32)
                for j in range(2):
                    r = blk * RB + i * 2 + j
                    oc = (o[:, j * 128 : (j + 1) * 128] * FAC).T
                    row = (r // 64) * 512 + info_ref[0] + r % 64
                    col = info_ref[1] + z * 128 + lax.broadcasted_iota(jnp.int32, (128, 128), 0)
                    o_ref[i * 2 + j] = jnp.where(col == row, 0.0, oc).astype(jnp.bfloat16)


def corr(rt, g, info):
    return pl.pallas_call(
        corr_kernel,
        grid=(4, NS1 + NS2),
        in_specs=[
            pl.BlockSpec(memory_space=pltpu.SMEM),
            pl.BlockSpec((128, 512), lambda z, t: (0, 0)),
            pl.BlockSpec((128, 256, 128), lambda z, t: (0, 0, 0)),
            pl.BlockSpec((2, 2, FB, 16, 128), lambda z, t: (z, 0, jnp.minimum(t, NS1 - 1), 0, 0)),
        ],
        out_specs=pl.BlockSpec((RB, 128, 128), lambda z, t: (jnp.maximum(t - NS1, 0), z, 0)),
        out_shape=jax.ShapeDtypeStruct((128, 512, 128), jnp.bfloat16),
        scratch_shapes=[pltpu.VMEM((256, 128, 2, 128), jnp.bfloat16)],
        compiler_params=pltpu.CompilerParams(vmem_limit_bytes=62 * 2**20),
    )(info, jnp.asarray(lag_np(), dtype=jnp.bfloat16), rt, g)


def body(samples, offsets):
    x = spectra(samples, offsets)
    g2, r = comm(x)
    rt = rows(r)
    info = jnp.stack([lax.axis_index("band") * 64, lax.axis_index("wide") * 512]).astype(jnp.int32)
    return corr(rt, g2, info).reshape(2, 64, 512, 128)


def solution(mesh):
    return jax.shard_map(
        body,
        mesh=mesh,
        in_specs=(P(None, "band", "wide"), P("wide")),
        out_specs=P(None, "band", "wide", None),
        check_vma=False,
    )
```

```python
import math

import jax
import jax.numpy as jnp
import ml_dtypes
import numpy as np
from jax import lax
from jax.experimental import pallas as pl
from jax.experimental.pallas import tpu as pltpu
from jax.sharding import PartitionSpec as P

MESH = pl.DeviceIdType.MESH
NQ = 4
NJ = 8
PW = 24
FAC = 1 / math.sqrt(32)


def dft_np():
    n=np.arange(512); f=np.arange(256)
    ph=(f[:,None]*n[None,:])%512
    ang=2*np.pi/512*ph
    win=0.5-0.5*np.cos(2*np.pi/512*(n+0.5))
    t=np.concatenate([np.cos(ang)*win, -np.sin(ang)*win],0).astype(ml_dtypes.bfloat16)
    t=t.reshape(2,32,8,512).transpose(1,0,2,3).reshape(512,512).astype(np.float32)
    return np.concatenate([t,np.zeros((512,128),np.float32)],1)

def lag_np():
    f=np.arange(256); l=np.arange(128)-64
    ph=(f[:,None]*l[None,:])%512
    ang=2*np.pi/512*ph
    t=np.concatenate([np.cos(ang)/16,-np.sin(ang)/16],0).astype(ml_dtypes.bfloat16)
    return t.reshape(2,256,128).transpose(2,1,0).reshape(128,512).copy()

def spec_kernel(off_ref, tab_ref, s_ref, x_ref, tk):
    i=pl.program_id(0)
    @pl.when(i==0)
    def _():
        for k in range(2):
            t=pltpu.roll(tab_ref[...], off_ref[k]+64*k, 1)
            tk[k]=t.astype(jnp.bfloat16)
    s=s_ref[...].reshape(128,1152)
    a0=lax.dot_general(tk[0], s[:, :640], (((1,),(1,)),((),())), preferred_element_type=jnp.float32)
    a1=lax.dot_general(tk[1], s[:, 512:], (((1,),(1,)),((),())), preferred_element_type=jnp.float32)
    lane=lax.broadcasted_iota(jnp.int32,(512,128),1)<64
    g0=jnp.where(lane,a0,pltpu.roll(a1,64,1))
    g1=jnp.where(lane,pltpu.roll(a0,64,1),a1)
    for j,g in enumerate((g0,g1)):
        v=g.reshape(32,2,8,128)
        re=v[:,0]; im=v[:,1]
        pw=re*re+im*im
        level=jnp.sum(jnp.sum(pw,0),0,keepdims=True)*(0.25/256.0)+1e-6
        inv=lax.rsqrt(pw+level[None])
        x_ref[j]=jnp.stack([re*inv,im*inv],1).reshape(32,16,128).astype(jnp.bfloat16)

def spectra(samples, offsets):
    return pl.pallas_call(spec_kernel,
      grid=(8,),
      in_specs=[pl.BlockSpec(memory_space=pltpu.SMEM), pl.BlockSpec((512,640),lambda i:(0,0)), pl.BlockSpec((2,64,1152),lambda i:(i,0,0))],
      out_specs=pl.BlockSpec((2,32,16,128),lambda i:(i,0,0,0)),
      out_shape=jax.ShapeDtypeStruct((16,32,16,128),jnp.bfloat16),
      scratch_shapes=[pltpu.VMEM((2,512,640),jnp.bfloat16)],
      compiler_params=pltpu.CompilerParams(vmem_limit_bytes=32*2**20),
    )(offsets, jnp.asarray(dft_np()), samples)

def relayout_quarter(rcv, tmp, hold, q):
    @pl.loop(0, 8)
    def _(fi):
        fg=q*8+fi
        for xs in range(2):
            for w in range(8):
                tmp[xs, w*PW:w*PW+16, :]=rcv[xs, w, fg].astype(jnp.float32)
        for xs in range(2):
            for f8 in range(8):
                re=tmp[xs, pl.ds(f8,8,stride=PW),:]
                im=tmp[xs, pl.ds(8+f8,8,stride=PW),:]
                hold[xs, fg*8+f8]=jnp.concatenate([re,im],0).astype(jnp.bfloat16)

def join2(a,b):
    return jnp.concatenate([a[:,:64],b[:,:64]],1), jnp.concatenate([a[:,64:],b[:,64:]],1)


def prep_rows(r_ref,fg,tmp,tt,rt):
    for w in range(16):
        y,xs,c=w//4,(w//2)%2,w%2
        for g in range(2):
            tmp[g,xs,(y*2+c)*PW:(y*2+c)*PW+16,:]=r_ref[w,g,fg].astype(jnp.float32)
    for fp in range(4):
        ks=[];ts=[]
        for f8 in (2*fp,2*fp+1):
            parts=[]
            for g in range(2):
                re=[tmp[g,xs,pl.ds(f8,8,stride=PW),:] for xs in range(2)]
                im=[tmp[g,xs,pl.ds(8+f8,8,stride=PW),:] for xs in range(2)]
                parts.append((jnp.concatenate([re[0],im[0],re[1],im[1]],0), jnp.concatenate([im[0],-re[0],im[1],-re[1]],0)))
            ks+=join2(parts[0][0],parts[1][0])
            ts+=join2(parts[0][1],parts[1][1])
        tt[fp,pl.ds(0,128,stride=2),:]=jnp.concatenate(ks,0).T
        tt[fp,pl.ds(1,128,stride=2),:]=jnp.concatenate(ts,0).T
        rt[fg*4+fp]=tt[fp].astype(jnp.bfloat16)


def stage_one(gs,rt,scr,f0,pairs):
    zero=jnp.zeros((64,128),jnp.bfloat16)
    for i in range(pairs):
        parts=[]
        for j in range(2):
            f=f0+2*i+j
            c=jnp.concatenate(join2(gs[0,:,f].reshape(32,128),gs[1,:,f].reshape(32,128)),0)
            parts.append(jnp.concatenate([c,zero] if j==0 else [zero,c],1))
        s=jnp.dot(rt[f0//2+i],jnp.concatenate(parts,0),preferred_element_type=jnp.float32)
        for j in range(2):
            scr[f0+2*i+j]=s[:,j*128:(j+1)*128].astype(jnp.bfloat16).reshape(128,2,128)


def stage_two(scr,lag,ost,slot_,r0,pairs,row_base,col_base):
    for i in range(pairs):
        rhs=jnp.concatenate([scr[:,r0+2*i+j].reshape(512,128) for j in range(2)],1)
        o=jnp.dot(lag,rhs,preferred_element_type=jnp.float32)
        for j in range(2):
            r=r0+2*i+j
            oc=(o[:,j*128:(j+1)*128]*FAC).T
            row=(r//64)*512+row_base+r%64
            col=col_base+lax.broadcasted_iota(jnp.int32,(128,128),0)
            ost[slot_,2*i+j]=jnp.where(col==row,0.0,oc).astype(jnp.bfloat16)


def main_kernel(x_ref, lag_ref, out_ref, g2_ref, rt_out, r_ref, rcv, tmp, hold, rtmp, tt, rt, gs, scr, ost,
                a_send, a_recv, r_send, r_recv, x_send, zp_send, zm_send, g_recv, l_sem, g_sem, o_sem, t_sem):
    wide=lax.axis_index("wide"); band=lax.axis_index("band")
    y=wide//4; xhi=(wide//2)%2; core=wide%2
    z=band//2; xl=band%2
    zp=(z+1)%4; zm=(z+3)%4; z2=(z+2)%4
    def wid(y_,xh_,c_): return (y_*2+xh_)*2+c_
    def a2a_dev(t):
        dy=t//4; dx=(t//2)%2; dc=t%2
        y_=(y+dy)%4; xh_=(xhi+dx)%2; c_=(core+dc)%2
        return y_,xh_,c_,dx
    dev_x=(wide, z*2+(1-xl)); dev_zp=(wide, zp*2+xl); dev_zm=(wide, zm*2+xl)
    dev_xhi=(wid(y,1-xhi,core), band)
    dev_core=(wid(y,xhi,1-core), band)
    bar=pltpu.get_barrier_semaphore()
    @pl.loop(1,16)
    def _(t):
        y_,xh_,c_,dx=a2a_dev(t)
        pl.semaphore_signal(bar,1,device_id=(wid(y_,xh_,c_), z*2+(xl+dx)%2),device_id_type=MESH)
    for d in (dev_x,dev_zp,dev_zm,dev_xhi):
        pl.semaphore_signal(bar,1,device_id=d,device_id_type=MESH)
    pl.semaphore_wait(bar,19)

    def rc(src,dst,ss,rs,dev):
        return pltpu.make_async_remote_copy(src_ref=src,dst_ref=dst,send_sem=ss,recv_sem=rs,device_id=dev,device_id_type=MESH)

    row_src=x_ref.at[pl.ds(0,2)]
    rows_xhi=rc(row_src, r_ref.at[wide], r_send.at[0], r_recv.at[wide], dev_xhi)
    rows_xhi.start()
    row_local=pltpu.make_async_copy(row_src, r_ref.at[wide], l_sem.at[0])
    row_local.start()
    own_local=pltpu.make_async_copy(x_ref.at[wide], rcv.at[xhi, y*2+core], l_sem.at[1])
    own_local.start()
    def a2a_copy(t,q):
        y_,xh_,c_,dx=a2a_dev(t)
        fs=pl.ds(q*8,8)
        return rc(x_ref.at[wid(y_,xh_,c_),fs], rcv.at[xhi,y*2+core,fs], a_send.at[t,q], a_recv.at[wide,q],
                  (wid(y_,xh_,c_), z*2+(xl+dx)%2))
    def a2a_wait(t,q):
        dy=t//4; dx=(t//2)%2; dc=t%2
        y_=(y+4-dy)%4; xh_=(xhi+dx)%2; c_=(core+dc)%2
        fs=pl.ds(q*8,8)
        s=wid(y_,xh_,c_)
        rc(x_ref.at[s,fs], rcv.at[xh_,y_*2+c_,fs], a_send.at[t,q], a_recv.at[s,q], dev_x).wait_recv()
    for q in range(NQ):
        @pl.loop(1,16)
        def _(t):
            a2a_copy(t,q).start()
    def row_y(dy,s,slot):
        return rc(r_ref.at[s], r_ref.at[s], r_send.at[slot], r_recv.at[s], (wid((y+dy)%4,xhi,core),band))
    def row_y_own(dy):
        return rc(row_src, r_ref.at[wide], r_send.at[dy], r_recv.at[wide], (wid((y+dy)%4,xhi,core),band))
    for dy in (1,2,3):
        row_y_own(dy).start()
    own_core=rc(row_src, r_ref.at[wide], r_send.at[4], r_recv.at[wide], dev_core)
    own_core.start()

    def slot(zz,xx,cls): return zz*2+(xx+cls)%2, (xhi+cls)%2
    def unit(b,xs,j): return g2_ref.at[b,xs,pl.ds(j*32,32)]
    def send(src,b,xs,j,sems,dev):
        return rc(src, unit(b,xs,j), sems.at[b,xs,j], g_recv.at[b,xs,j], dev)
    def wait_unit(zz,xx,cls,j):
        b,xs=slot(zz,xx,cls)
        send(unit(b,xs,j),b,xs,j,x_send,dev_x).wait_recv()
        return b,xs
    own_local.wait()
    for q in range(NQ):
        @pl.loop(1,16)
        def _(t):
            a2a_wait(t,q)
        relayout_quarter(rcv,tmp,hold,q)
        @pl.loop(q*2,q*2+2)
        def _(j):
            for cls in range(2):
                b,xs=slot(z,xl,cls)
                src=hold.at[xs,pl.ds(j*32,32)]
                send(src,b,xs,j,x_send,dev_x).start()
                send(src,b,xs,j,zp_send,dev_zp).start()
                send(src,b,xs,j,zm_send,dev_zm).start()
                pltpu.make_async_copy(src,unit(b,xs,j),l_sem.at[2+cls*8+j]).start()
    ps=wid(y,1-xhi,core)
    rc(row_src,r_ref.at[ps],r_send.at[0],r_recv.at[ps],dev_x).wait_recv()
    for dy in (1,2,3):
        row_y(dy,ps,4+dy).start()
    rc(r_ref.at[ps],r_ref.at[ps],r_send.at[8],r_recv.at[ps],dev_core).start()
    def pass_core(dy,xh_,slot_):
        s=wid((y+dy)%4,xh_,core)
        rc(row_src,r_ref.at[s],r_send.at[0],r_recv.at[s],dev_x).wait_recv()
        rc(r_ref.at[s],r_ref.at[s],r_send.at[slot_],r_recv.at[s],dev_core).start()
    for dy in (1,3,2):
        pass_core(dy,xhi,8+dy)
    for dy in (1,3,2):
        pass_core(dy,1-xhi,11+dy)
    for dy in range(4):
        for xh_ in range(2):
            s=wid((y+dy)%4,xh_,1-core)
            rc(row_src,r_ref.at[s],r_send.at[0],r_recv.at[s],dev_x).wait_recv()
    row_local.wait()

    def put(b,xs,j,sems,dev):
        send(unit(b,xs,j),b,xs,j,sems,dev).start()

    def near(j):
        b,xs=wait_unit(z,1-xl,0,j)
        put(b,xs,j,zp_send,dev_zp)
        put(b,xs,j,zm_send,dev_zm)
        b2,xs2=wait_unit(zp,xl,1,j)
        @pl.when(j<7)
        def _():
            put(b2,xs2,j,x_send,dev_x)
        @pl.when(j==7)
        def _():
            b1,xs1=wait_unit(z,1-xl,1,j)
            put(b1,xs1,j,zp_send,dev_zp)
            put(b1,xs1,j,zm_send,dev_zm)

    @pl.loop(0,32)
    def _(fg):
        prep_rows(r_ref,fg,rtmp,tt,rt)
        @pl.when(fg%4==3)
        def _():
            near(fg//4)
    rt_copy=pltpu.make_async_copy(rt,rt_out,t_sem)
    rt_copy.start()

    def pass_on(j):
        b,xs=wait_unit(zm,xl,1,j)
        @pl.when(j<7)
        def _():
            put(b,xs,j,x_send,dev_x)
        b1,xs1=wait_unit(zm,xl,0,j)
        b2,xs2=wait_unit(zp,xl,0,j)
        b3,xs3=slot(zp,xl,1)
        @pl.when(j%2==0)
        def _():
            put(b,xs,j,zp_send,dev_zp)
            put(b1,xs1,j,zp_send,dev_zp)
        @pl.when(j%2==1)
        def _():
            put(b2,xs2,j,zm_send,dev_zm)
            put(b3,xs3,j,zm_send,dev_zm)

    def far(j):
        b,xs=wait_unit(z2,xl,1,j)
        @pl.when(j<7)
        def _():
            put(b,xs,j,x_send,dev_x)

    def across(zz):
        @pl.loop(0,7)
        def _(j):
            wait_unit(zz,1-xl,1,j)

    def relay():
        @pl.loop(0,NJ)
        def _(j):
            for zz,parity,sems,dev in ((zm,0,zp_send,dev_zp),(zp,1,zm_send,dev_zm)):
                b,xs=wait_unit(zz,1-xl,0,j)
                @pl.when(j%2==parity)
                def _():
                    put(b,xs,j,sems,dev)
                @pl.when(j==7)
                def _():
                    b1,xs1=wait_unit(zz,1-xl,1,j)
                    if parity==1:
                        put(b1,xs1,j,sems,dev)

    @pl.loop(0,NJ)
    def _(j):
        for cls in range(2):
            b,xs=slot(z,xl,cls)
            pltpu.make_async_copy(hold.at[xs,pl.ds(j*32,32)],unit(b,xs,j),l_sem.at[2+cls*8+j]).wait()
    lag=lag_ref[...]
    @pl.loop(0,3)
    def _(s):
        zz=(z+s+s//2)%4
        @pl.when(s==0)
        def _():
            across(z)
        @pl.when(s==1)
        def _():
            relay()
            across(zp)
        @pl.when(s==2)
        def _():
            across(zm)
        def g_copy(j):
            fs=pl.ds(j*32,32)
            return pltpu.make_async_copy(g2_ref.at[pl.ds(zz*2,2),:,fs],gs.at[:,:,fs],g_sem.at[j])
        for j in range(NJ):
            g_copy(j).start()
        @pl.loop(0,NJ)
        def _(j):
            @pl.when(s==0)
            def _():
                pass_on(j)
            g_copy(j).wait()
            @pl.loop(0,2)
            def _(i0):
                stage_one(gs,rt,scr,j*32+i0*16,8)
        def o_copy(i):
            return pltpu.make_async_copy(ost.at[i%2],out_ref.at[s,pl.ds(i*16,16)],o_sem.at[i%2])
        @pl.loop(0,8)
        def _(i):
            @pl.when(s==1)
            def _():
                far(i)
            @pl.when(i>=2)
            def _():
                o_copy(i).wait()
            stage_two(scr,lag,ost,i%2,i*16,8,band*64,wide*512+zz*128)
            o_copy(i).start()
        o_copy(0).wait()
        o_copy(1).wait()

    @pl.loop(0,NJ)
    def _(j):
        wait_unit(z2,xl,0,j)
        wait_unit(z2,1-xl,0,j)
        wait_unit(z2,1-xl,1,j)
    rt_copy.wait()
    for i in range(15):
        rc(row_src,r_ref.at[wide],r_send.at[i],r_recv.at[wide],dev_x).wait_send()
    @pl.loop(1,16)
    def _(t):
        for q in range(NQ):
            a2a_copy(t,q).wait_send()
    def ws(zz,xx,cls,j,sems):
        b,xs=slot(zz,xx,cls)
        send(unit(b,xs,j),b,xs,j,sems,dev_x).wait_send()
    @pl.loop(0,NJ)
    def _(j):
        for cls in range(2):
            b,xs=slot(z,xl,cls)
            ws(z,xl,cls,j,x_send)
            ws(z,xl,cls,j,zp_send); ws(z,xl,cls,j,zm_send)
        ws(z,1-xl,0,j,zp_send); ws(z,1-xl,0,j,zm_send)
        @pl.when(j==7)
        def _():
            ws(z,1-xl,1,j,zp_send); ws(z,1-xl,1,j,zm_send)
        @pl.when(j<7)
        def _():
            for zz in (zm,zp,z2): ws(zz,xl,1,j,x_send)
        for zz,parity,sems in ((zm,0,zp_send),(zp,1,zm_send)):
            @pl.when(j%2==parity)
            def _():
                ws(zz,xl,0,j,sems); ws(zz,xl,1,j,sems); ws(zz,1-xl,0,j,sems)
            if parity==1:
                @pl.when(j==7)
                def _(): ws(zz,1-xl,1,j,sems)


def main(x,lag):
    D=pltpu.SemaphoreType.DMA
    A=pl.BlockSpec(memory_space=pl.ANY)
    bf=jnp.bfloat16
    return pl.pallas_call(main_kernel,
      in_specs=[A,pl.BlockSpec(memory_space=pltpu.VMEM)],
      out_specs=[A]*3,
      out_shape=[jax.ShapeDtypeStruct((3,128,128,128),bf),jax.ShapeDtypeStruct((8,2,256,16,128),bf),jax.ShapeDtypeStruct((128,256,128),bf)],
      scratch_shapes=[pltpu.VMEM((16,2,32,16,128),bf),pltpu.VMEM((2,8,32,16,128),bf),pltpu.VMEM((2,8*PW,128),jnp.float32),pltpu.VMEM((2,256,16,128),bf),
        pltpu.VMEM((2,2,8*PW,128),jnp.float32),pltpu.VMEM((4,256,128),jnp.float32),pltpu.VMEM((128,256,128),bf),
        pltpu.VMEM((2,2,256,16,128),bf),pltpu.VMEM((256,128,2,128),bf),pltpu.VMEM((2,16,128,128),bf),
        D((16,4)),D((16,4)),D((16,)),D((16,)),D((8,2,8)),D((8,2,8)),D((8,2,8)),D((8,2,8)),D((18,)),D((8,)),D((2,)),D(())],
      compiler_params=pltpu.CompilerParams(collective_id=0,has_side_effects=True,vmem_limit_bytes=60*2**20),
    )(x,lag)


def last_kernel(info_ref,lag_ref,rt_ref,g_ref,done_ref,out_ref,scr,ost,buf,c_sem,o_sem):
    t=pl.program_id(0)
    z=info_ref[2]
    far=(z+2)%4
    def take(c):
        return pltpu.make_async_copy(done_ref.at[c//4,pl.ds((c%4)*32,32)],buf.at[c%2],c_sem.at[0,c%2])
    def give(c):
        s=c//4
        return pltpu.make_async_copy(buf.at[c%2],out_ref.at[pl.ds((c%4)*32,32),(z+s+s//2)%4],c_sem.at[1,c%2])
    @pl.when(t==0)
    def _():
        take(0).start()
    take(t).wait()
    @pl.when(t>=1)
    def _():
        give(t-1).wait()
    @pl.when(t<11)
    def _():
        take(t+1).start()
    give(t).start()
    @pl.when(t<4)
    def _():
        @pl.loop(0,2)
        def _(i0):
            for i in range(16):
                parts=[]
                zero=jnp.zeros((64,128),jnp.bfloat16)
                for j in range(2):
                    f=i0*32+2*i+j
                    c=jnp.concatenate(join2(g_ref[0,:,f].reshape(32,128),g_ref[1,:,f].reshape(32,128)),0)
                    parts.append(jnp.concatenate([c,zero] if j==0 else [zero,c],1))
                s=jnp.dot(rt_ref[i0*16+i],jnp.concatenate(parts,0),preferred_element_type=jnp.float32)
                for j in range(2):
                    scr[t*64+i0*32+2*i+j]=s[:,j*128:(j+1)*128].astype(jnp.bfloat16).reshape(128,2,128)
    @pl.when(t>=4)
    def _():
        i=t-4
        def o_copy(i):
            return pltpu.make_async_copy(ost.at[i%2],out_ref.at[pl.ds(i*16,16),far],o_sem.at[i%2])
        @pl.when(i>=2)
        def _():
            o_copy(i).wait()
        stage_two(scr,lag_ref[...],ost,i%2,i*16,8,info_ref[0],info_ref[1]+far*128)
        o_copy(i).start()
        @pl.when(i==7)
        def _():
            o_copy(0).wait()
            o_copy(1).wait()
            give(11).wait()


def last(info,lag,rt,g2,done):
    D=pltpu.SemaphoreType.DMA
    A=pl.BlockSpec(memory_space=pl.ANY)
    q=lambda t: jnp.minimum(t,3)
    return pl.pallas_call(last_kernel,
      grid_spec=pltpu.PrefetchScalarGridSpec(num_scalar_prefetch=1,grid=(12,),
        in_specs=[pl.BlockSpec((128,512),lambda t,i:(0,0)),
          pl.BlockSpec((32,256,128),lambda t,i:(q(t),0,0)),
          pl.BlockSpec((2,2,64,16,128),lambda t,i:((i[2]+2)%4,0,q(t),0,0)),A],
        out_specs=A,
        scratch_shapes=[pltpu.VMEM((256,128,2,128),jnp.bfloat16),pltpu.VMEM((2,16,128,128),jnp.bfloat16),pltpu.VMEM((2,32,128,128),jnp.bfloat16),D((2,2)),D((2,))]),
      out_shape=jax.ShapeDtypeStruct((128,4,128,128),jnp.bfloat16),
      compiler_params=pltpu.CompilerParams(vmem_limit_bytes=60*2**20),
    )(info,lag,rt,g2,done)


def body(samples, offsets):
    x = spectra(samples, offsets)
    lag = jnp.asarray(lag_np(), dtype=jnp.bfloat16)
    done, g2, rt = main(x, lag)
    band = lax.axis_index("band")
    info = jnp.stack([band * 64, lax.axis_index("wide") * 512, band // 2]).astype(jnp.int32)
    return last(info, lag, rt, g2, done).reshape(2, 64, 512, 128)


def solution(mesh):
    return jax.shard_map(
        body,
        mesh=mesh,
        in_specs=(P(None, "band", "wide"), P("wide")),
        out_specs=P(None, "band", "wide", None),
        check_vma=False,
    )
```

```python
import math

import jax
import jax.numpy as jnp
import ml_dtypes
import numpy as np
from jax import lax
from jax.experimental import pallas as pl
from jax.experimental.pallas import tpu as pltpu
from jax.sharding import PartitionSpec as P

MESH = pl.DeviceIdType.MESH
NQ = 4
NJ = 8
PW = 24
NA = 7
PITCH = 264
FAC = 1 / math.sqrt(32)


def dft_np():
    n=np.arange(512); f=np.arange(256)
    ph=(f[:,None]*n[None,:])%512
    ang=2*np.pi/512*ph
    win=0.5-0.5*np.cos(2*np.pi/512*(n+0.5))
    t=np.concatenate([np.cos(ang)*win, -np.sin(ang)*win],0).astype(ml_dtypes.bfloat16)
    t=t.reshape(2,32,8,512).transpose(1,0,2,3).reshape(512,512).astype(np.float32)
    return np.concatenate([t,np.zeros((512,128),np.float32)],1)

def lag_np():
    f=np.arange(256); l=np.arange(128)-64
    ph=(f[:,None]*l[None,:])%512
    ang=2*np.pi/512*ph
    t=np.concatenate([np.cos(ang)/16,-np.sin(ang)/16],0).astype(ml_dtypes.bfloat16)
    return t.T.copy()

def spec_kernel(off_ref, tab_ref, s_ref, x_ref, tk):
    i=pl.program_id(0)
    @pl.when(i==0)
    def _():
        for k in range(2):
            t=pltpu.roll(tab_ref[...], off_ref[k]+64*k, 1)
            tk[k]=t.astype(jnp.bfloat16)
    s=s_ref[...].reshape(128,1152)
    a0=lax.dot_general(tk[0], s[:, :640], (((1,),(1,)),((),())), preferred_element_type=jnp.float32)
    a1=lax.dot_general(tk[1], s[:, 512:], (((1,),(1,)),((),())), preferred_element_type=jnp.float32)
    lane=lax.broadcasted_iota(jnp.int32,(512,128),1)<64
    g0=jnp.where(lane,a0,pltpu.roll(a1,64,1))
    g1=jnp.where(lane,pltpu.roll(a0,64,1),a1)
    for j,g in enumerate((g0,g1)):
        v=g.reshape(32,2,8,128)
        re=v[:,0]; im=v[:,1]
        pw=re*re+im*im
        level=jnp.sum(jnp.sum(pw,0),0,keepdims=True)*(0.25/256.0)+1e-6
        inv=lax.rsqrt(pw+level[None])
        x_ref[j]=jnp.stack([re*inv,im*inv],1).reshape(32,16,128).astype(jnp.bfloat16)

def spectra(samples, offsets):
    return pl.pallas_call(spec_kernel,
      grid=(8,),
      in_specs=[pl.BlockSpec(memory_space=pltpu.SMEM), pl.BlockSpec((512,640),lambda i:(0,0)), pl.BlockSpec((2,64,1152),lambda i:(i,0,0))],
      out_specs=pl.BlockSpec((2,32,16,128),lambda i:(i,0,0,0)),
      out_shape=jax.ShapeDtypeStruct((16,32,16,128),jnp.bfloat16),
      scratch_shapes=[pltpu.VMEM((2,512,640),jnp.bfloat16)],
      compiler_params=pltpu.CompilerParams(vmem_limit_bytes=32*2**20),
    )(offsets, jnp.asarray(dft_np()), samples)

def relayout_quarter(rcv, tmp, hold, q):
    @pl.loop(0, 8)
    def _(fi):
        fg=q*8+fi
        for xs in range(2):
            for w in range(8):
                tmp[xs, w*PW:w*PW+16, :]=rcv[xs, w, fg].astype(jnp.float32)
        for xs in range(2):
            for f8 in range(8):
                re=tmp[xs, pl.ds(f8,8,stride=PW),:]
                im=tmp[xs, pl.ds(8+f8,8,stride=PW),:]
                hold[xs, fg*8+f8]=jnp.concatenate([re,im],0).astype(jnp.bfloat16)

def join2(a,b):
    return jnp.concatenate([a[:,:64],b[:,:64]],1), jnp.concatenate([a[:,64:],b[:,64:]],1)


def prep_rows(r_ref,fg,tmp,rt):
    for w in range(16):
        y,xs,c=w//4,(w//2)%2,w%2
        for g in range(2):
            tmp[g,xs,(y*2+c)*PW:(y*2+c)*PW+16,:]=r_ref[w,g,fg].astype(jnp.float32)
    for fp in range(4):
        ks=[];ts=[]
        for f8 in (2*fp,2*fp+1):
            parts=[]
            for g in range(2):
                re=[tmp[g,xs,pl.ds(f8,8,stride=PW),:] for xs in range(2)]
                im=[tmp[g,xs,pl.ds(8+f8,8,stride=PW),:] for xs in range(2)]
                parts.append((jnp.concatenate([re[0],im[0],re[1],im[1]],0), jnp.concatenate([im[0],-re[0],im[1],-re[1]],0)))
            ks+=join2(parts[0][0],parts[1][0])
            ts+=join2(parts[0][1],parts[1][1])
        rt[fg*4+fp,0:128]=jnp.concatenate(ks,0).T.astype(jnp.bfloat16)
        rt[fg*4+fp,128:256]=jnp.concatenate(ts,0).T.astype(jnp.bfloat16)


def stage_one(gs,rt,scr,f0,pairs):
    zero=jnp.zeros((64,128),jnp.bfloat16)
    for i in range(pairs):
        parts=[]
        for j in range(2):
            f=f0+2*i+j
            c=jnp.concatenate(join2(gs[0,:,f].reshape(32,128),gs[1,:,f].reshape(32,128)),0)
            parts.append(jnp.concatenate([c,zero] if j==0 else [zero,c],1))
        s=jnp.dot(rt[f0//2+i],jnp.concatenate(parts,0),preferred_element_type=jnp.float32)
        for j in range(2):
            scr[pl.ds(pl.multiple_of((f0+2*i+j)*PITCH,8),256),:]=s[:,j*128:(j+1)*128]


def stage_two(scr,lag,ost,slot_,r0,pairs,row_base,col_base):
    for i in range(pairs):
        rows=[r0+2*i+j for j in range(2)]
        rhs=jnp.concatenate([jnp.concatenate([scr[pl.ds(p*128+r,256,stride=PITCH),:].astype(jnp.bfloat16) for p in range(2)],0) for r in rows],1)
        o=jnp.dot(lag,rhs,preferred_element_type=jnp.float32)
        for j in range(2):
            r=r0+2*i+j
            oc=(o[:,j*128:(j+1)*128]*FAC).T
            row=(r//64)*512+row_base+r%64
            col=col_base+lax.broadcasted_iota(jnp.int32,(128,128),0)
            ost[slot_,2*i+j]=jnp.where(col==row,0.0,oc).astype(jnp.bfloat16)


def main_kernel(x_ref, lag_ref, out_ref, g2_ref, rt_out, r_ref, rcv, tmp, hold, rtmp, rt, gs, scr, ost,
                a_send, a_recv, r_send, r_recv, x_send, zp_send, zm_send, g_recv, l_sem, g_sem, o_sem, t_sem):
    wide=lax.axis_index("wide"); band=lax.axis_index("band")
    y=wide//4; xhi=(wide//2)%2; core=wide%2
    z=band//2; xl=band%2
    zp=(z+1)%4; zm=(z+3)%4; z2=(z+2)%4
    def wid(y_,xh_,c_): return (y_*2+xh_)*2+c_
    def a2a_dev(t):
        dy=t//4; dx=(t//2)%2; dc=t%2
        y_=(y+dy)%4; xh_=(xhi+dx)%2; c_=(core+dc)%2
        return y_,xh_,c_,dx
    dev_x=(wide, z*2+(1-xl)); dev_zp=(wide, zp*2+xl); dev_zm=(wide, zm*2+xl)
    dev_xhi=(wid(y,1-xhi,core), band)
    dev_core=(wid(y,xhi,1-core), band)
    bar=pltpu.get_barrier_semaphore()
    @pl.loop(1,16)
    def _(t):
        y_,xh_,c_,dx=a2a_dev(t)
        pl.semaphore_signal(bar,1,device_id=(wid(y_,xh_,c_), z*2+(xl+dx)%2),device_id_type=MESH)
    for d in (dev_x,dev_zp,dev_zm,dev_xhi):
        pl.semaphore_signal(bar,1,device_id=d,device_id_type=MESH)
    pl.semaphore_wait(bar,19)

    def rc(src,dst,ss,rs,dev):
        return pltpu.make_async_remote_copy(src_ref=src,dst_ref=dst,send_sem=ss,recv_sem=rs,device_id=dev,device_id_type=MESH)

    row_src=x_ref.at[pl.ds(0,2)]
    rows_xhi=rc(row_src, r_ref.at[wide], r_send.at[0], r_recv.at[wide], dev_xhi)
    row_local=pltpu.make_async_copy(row_src, r_ref.at[wide], l_sem.at[0])
    row_local.start()
    own_local=pltpu.make_async_copy(x_ref.at[wide], rcv.at[xhi, y*2+core], l_sem.at[1])
    own_local.start()
    def a2a_copy(t,q):
        y_,xh_,c_,dx=a2a_dev(t)
        fs=pl.ds(q*8,8)
        return rc(x_ref.at[wid(y_,xh_,c_),fs], rcv.at[xhi,y*2+core,fs], a_send.at[t,q], a_recv.at[wide,q],
                  (wid(y_,xh_,c_), z*2+(xl+dx)%2))
    def a2a_wait(t,q):
        dy=t//4; dx=(t//2)%2; dc=t%2
        y_=(y+4-dy)%4; xh_=(xhi+dx)%2; c_=(core+dc)%2
        fs=pl.ds(q*8,8)
        s=wid(y_,xh_,c_)
        rc(x_ref.at[s,fs], rcv.at[xh_,y_*2+c_,fs], a_send.at[t,q], a_recv.at[s,q], dev_x).wait_recv()
    for q in range(2):
        @pl.loop(1,16)
        def _(t):
            a2a_copy(t,q).start()
    def row_y(dy,s,slot):
        return rc(r_ref.at[s], r_ref.at[s], r_send.at[slot], r_recv.at[s], (wid((y+dy)%4,xhi,core),band))
    def row_y_own(dy):
        return rc(row_src, r_ref.at[wide], r_send.at[dy], r_recv.at[wide], (wid((y+dy)%4,xhi,core),band))
    own_core=rc(row_src, r_ref.at[wide], r_send.at[4], r_recv.at[wide], dev_core)

    def slot(zz,xx,cls): return zz*2+(xx+cls)%2, (xhi+cls)%2
    def unit(b,xs,j): return g2_ref.at[b,xs,pl.ds(j*32,32)]
    def send(src,b,xs,j,sems,dev):
        return rc(src, unit(b,xs,j), sems.at[b,xs,j], g_recv.at[b,xs,j], dev)
    def wait_unit(zz,xx,cls,j):
        b,xs=slot(zz,xx,cls)
        send(unit(b,xs,j),b,xs,j,x_send,dev_x).wait_recv()
        return b,xs
    own_local.wait()
    for q in range(NQ):
        @pl.loop(1,16)
        def _(t):
            a2a_wait(t,q)
        relayout_quarter(rcv,tmp,hold,q)
        @pl.loop(q*2,q*2+2)
        def _(j):
            for cls in range(2):
                b,xs=slot(z,xl,cls)
                src=hold.at[xs,pl.ds(j*32,32)]
                send(src,b,xs,j,x_send,dev_x).start()
                send(src,b,xs,j,zp_send,dev_zp).start()
                send(src,b,xs,j,zm_send,dev_zm).start()
                pltpu.make_async_copy(src,unit(b,xs,j),l_sem.at[2+cls*8+j]).start()
        if q+2<NQ:
            @pl.loop(1,16)
            def _(t):
                a2a_copy(t,q+2).start()
        if q==1:
            rows_xhi.start()
        if q==2:
            for dy in (1,2,3):
                row_y_own(dy).start()
            own_core.start()
    ps=wid(y,1-xhi,core)
    rc(row_src,r_ref.at[ps],r_send.at[0],r_recv.at[ps],dev_x).wait_recv()
    for dy in (1,2,3):
        row_y(dy,ps,4+dy).start()
    rc(r_ref.at[ps],r_ref.at[ps],r_send.at[8],r_recv.at[ps],dev_core).start()
    def pass_core(dy,xh_,slot_):
        s=wid((y+dy)%4,xh_,core)
        rc(row_src,r_ref.at[s],r_send.at[0],r_recv.at[s],dev_x).wait_recv()
        rc(r_ref.at[s],r_ref.at[s],r_send.at[slot_],r_recv.at[s],dev_core).start()
    for dy in (1,3,2):
        pass_core(dy,xhi,8+dy)
    for dy in (1,3,2):
        pass_core(dy,1-xhi,11+dy)
    for dy in range(4):
        for xh_ in range(2):
            s=wid((y+dy)%4,xh_,1-core)
            rc(row_src,r_ref.at[s],r_send.at[0],r_recv.at[s],dev_x).wait_recv()
    row_local.wait()

    def put(b,xs,j,sems,dev):
        send(unit(b,xs,j),b,xs,j,sems,dev).start()

    def near(j):
        b,xs=wait_unit(z,1-xl,0,j)
        put(b,xs,j,zp_send,dev_zp)
        put(b,xs,j,zm_send,dev_zm)
        b2,xs2=wait_unit(zp,xl,1,j)
        @pl.when(j<NA)
        def _():
            put(b2,xs2,j,x_send,dev_x)
        @pl.when(j>=NA)
        def _():
            b1,xs1=wait_unit(z,1-xl,1,j)
            put(b1,xs1,j,zp_send,dev_zp)
            put(b1,xs1,j,zm_send,dev_zm)

    @pl.loop(0,32)
    def _(fg):
        prep_rows(r_ref,fg,rtmp,rt)
        @pl.when(fg%4==3)
        def _():
            near(fg//4)
    rt_copy=pltpu.make_async_copy(rt,rt_out,t_sem)
    rt_copy.start()

    def pass_on(j):
        b,xs=wait_unit(zm,xl,1,j)
        @pl.when(j<NA)
        def _():
            put(b,xs,j,x_send,dev_x)
        @pl.when(j%2==0)
        def _():
            put(b,xs,j,zp_send,dev_zp)
        b3,xs3=slot(zp,xl,1)
        @pl.when(j%2==1)
        def _():
            put(b3,xs3,j,zm_send,dev_zm)

    def pass_own(j):
        b1,xs1=wait_unit(zm,xl,0,j)
        b2,xs2=wait_unit(zp,xl,0,j)
        @pl.when(j%2==0)
        def _():
            put(b1,xs1,j,zp_send,dev_zp)
        @pl.when(j%2==1)
        def _():
            put(b2,xs2,j,zm_send,dev_zm)

    def far(j):
        b,xs=wait_unit(z2,xl,1,j)
        @pl.when(j<NA)
        def _():
            put(b,xs,j,x_send,dev_x)

    def across(zz):
        @pl.loop(0,NA)
        def _(j):
            wait_unit(zz,1-xl,1,j)

    def relay():
        @pl.loop(0,NJ)
        def _(j):
            for zz,parity,sems,dev in ((zm,0,zp_send,dev_zp),(zp,1,zm_send,dev_zm)):
                b,xs=wait_unit(zz,1-xl,0,j)
                @pl.when(j%2==parity)
                def _():
                    put(b,xs,j,sems,dev)
                @pl.when(j>=NA)
                def _():
                    b1,xs1=wait_unit(zz,1-xl,1,j)
                    @pl.when(j%2==parity)
                    def _():
                        put(b1,xs1,j,sems,dev)

    @pl.loop(0,NJ)
    def _(j):
        for cls in range(2):
            b,xs=slot(z,xl,cls)
            pltpu.make_async_copy(hold.at[xs,pl.ds(j*32,32)],unit(b,xs,j),l_sem.at[2+cls*8+j]).wait()
    lag=lag_ref[...]
    @pl.loop(0,3)
    def _(s):
        zz=(z+s+s//2)%4
        @pl.when(s==0)
        def _():
            across(z)
        @pl.when(s==1)
        def _():
            relay()
            across(zp)
        @pl.when(s==2)
        def _():
            across(zm)
        def g_copy(j):
            fs=pl.ds(j*32,32)
            return pltpu.make_async_copy(g2_ref.at[pl.ds(zz*2,2),:,fs],gs.at[:,:,fs],g_sem.at[j])
        for j in range(NJ):
            g_copy(j).start()
        @pl.loop(0,NJ)
        def _(j):
            @pl.when(s==0)
            def _():
                pass_on(j)
            g_copy(j).wait()
            stage_one(gs,rt,scr,j*32,16)
        def o_copy(i):
            return pltpu.make_async_copy(ost.at[i%2],out_ref.at[s,pl.ds(i*16,16)],o_sem.at[i%2])
        @pl.loop(0,8)
        def _(i):
            @pl.when(s==0)
            def _():
                pass_own(i)
            @pl.when(s==1)
            def _():
                far(i)
            @pl.when(i>=2)
            def _():
                o_copy(i).wait()
            stage_two(scr,lag,ost,i%2,i*16,8,band*64,wide*512+zz*128)
            o_copy(i).start()
        o_copy(0).wait()
        o_copy(1).wait()

    @pl.loop(0,NJ)
    def _(j):
        wait_unit(z2,xl,0,j)
        wait_unit(z2,1-xl,0,j)
        wait_unit(z2,1-xl,1,j)
    rt_copy.wait()
    for i in range(15):
        rc(row_src,r_ref.at[wide],r_send.at[i],r_recv.at[wide],dev_x).wait_send()
    @pl.loop(1,16)
    def _(t):
        for q in range(NQ):
            a2a_copy(t,q).wait_send()
    def ws(zz,xx,cls,j,sems):
        b,xs=slot(zz,xx,cls)
        send(unit(b,xs,j),b,xs,j,sems,dev_x).wait_send()
    @pl.loop(0,NJ)
    def _(j):
        for cls in range(2):
            b,xs=slot(z,xl,cls)
            ws(z,xl,cls,j,x_send)
            ws(z,xl,cls,j,zp_send); ws(z,xl,cls,j,zm_send)
        ws(z,1-xl,0,j,zp_send); ws(z,1-xl,0,j,zm_send)
        @pl.when(j>=NA)
        def _():
            ws(z,1-xl,1,j,zp_send); ws(z,1-xl,1,j,zm_send)
        @pl.when(j<NA)
        def _():
            for zz in (zm,zp,z2): ws(zz,xl,1,j,x_send)
        for zz,parity,sems in ((zm,0,zp_send),(zp,1,zm_send)):
            @pl.when(j%2==parity)
            def _():
                ws(zz,xl,0,j,sems); ws(zz,xl,1,j,sems); ws(zz,1-xl,0,j,sems)
                @pl.when(j>=NA)
                def _():
                    ws(zz,1-xl,1,j,sems)


def main(x,lag):
    D=pltpu.SemaphoreType.DMA
    A=pl.BlockSpec(memory_space=pl.ANY)
    bf=jnp.bfloat16
    return pl.pallas_call(main_kernel,
      in_specs=[A,pl.BlockSpec(memory_space=pltpu.VMEM)],
      out_specs=[A]*3,
      out_shape=[jax.ShapeDtypeStruct((3,128,128,128),bf),jax.ShapeDtypeStruct((8,2,256,16,128),bf),jax.ShapeDtypeStruct((128,256,128),bf)],
      scratch_shapes=[pltpu.VMEM((16,2,32,16,128),bf),pltpu.VMEM((2,8,32,16,128),bf),pltpu.VMEM((2,8*PW,128),jnp.float32),pltpu.VMEM((2,256,16,128),bf),
        pltpu.VMEM((2,2,8*PW,128),jnp.float32),pltpu.VMEM((128,256,128),bf),
        pltpu.VMEM((2,2,256,16,128),bf),pltpu.VMEM((256*PITCH,128),jnp.float32),pltpu.VMEM((2,16,128,128),bf),
        D((16,4)),D((16,4)),D((16,)),D((16,)),D((8,2,8)),D((8,2,8)),D((8,2,8)),D((8,2,8)),D((18,)),D((8,)),D((2,)),D(())],
      compiler_params=pltpu.CompilerParams(collective_id=0,has_side_effects=True,vmem_limit_bytes=60*2**20),
    )(x,lag)


def last_kernel(info_ref,lag_ref,rt_ref,g_ref,done_ref,out_ref,scr,ost,buf,c_sem,o_sem):
    t=pl.program_id(0)
    z=info_ref[2]
    far=(z+2)%4
    def take(c):
        return pltpu.make_async_copy(done_ref.at[c//4,pl.ds((c%4)*32,32)],buf.at[c%2],c_sem.at[0,c%2])
    def give(c):
        s=c//4
        return pltpu.make_async_copy(buf.at[c%2],out_ref.at[pl.ds((c%4)*32,32),(z+s+s//2)%4],c_sem.at[1,c%2])
    @pl.when(t==0)
    def _():
        take(0).start()
    take(t).wait()
    @pl.when(t>=1)
    def _():
        give(t-1).wait()
    @pl.when(t<11)
    def _():
        take(t+1).start()
    give(t).start()
    @pl.when(t<4)
    def _():
        @pl.loop(0,2)
        def _(i0):
            for i in range(16):
                parts=[]
                zero=jnp.zeros((64,128),jnp.bfloat16)
                for j in range(2):
                    f=i0*32+2*i+j
                    c=jnp.concatenate(join2(g_ref[0,:,f].reshape(32,128),g_ref[1,:,f].reshape(32,128)),0)
                    parts.append(jnp.concatenate([c,zero] if j==0 else [zero,c],1))
                s=jnp.dot(rt_ref[i0*16+i],jnp.concatenate(parts,0),preferred_element_type=jnp.float32)
                for j in range(2):
                    scr[pl.ds(pl.multiple_of((t*64+i0*32+2*i+j)*PITCH,8),256),:]=s[:,j*128:(j+1)*128]
    @pl.when(t>=4)
    def _():
        i=t-4
        def o_copy(i):
            return pltpu.make_async_copy(ost.at[i%2],out_ref.at[pl.ds(i*16,16),far],o_sem.at[i%2])
        @pl.when(i>=2)
        def _():
            o_copy(i).wait()
        stage_two(scr,lag_ref[...],ost,i%2,i*16,8,info_ref[0],info_ref[1]+far*128)
        o_copy(i).start()
        @pl.when(i==7)
        def _():
            o_copy(0).wait()
            o_copy(1).wait()
            give(11).wait()


def last(info,lag,rt,g2,done):
    D=pltpu.SemaphoreType.DMA
    A=pl.BlockSpec(memory_space=pl.ANY)
    q=lambda t: jnp.minimum(t,3)
    return pl.pallas_call(last_kernel,
      grid_spec=pltpu.PrefetchScalarGridSpec(num_scalar_prefetch=1,grid=(12,),
        in_specs=[pl.BlockSpec((128,512),lambda t,i:(0,0)),
          pl.BlockSpec((32,256,128),lambda t,i:(q(t),0,0)),
          pl.BlockSpec((2,2,64,16,128),lambda t,i:((i[2]+2)%4,0,q(t),0,0)),A],
        out_specs=A,
        scratch_shapes=[pltpu.VMEM((256*PITCH,128),jnp.float32),pltpu.VMEM((2,16,128,128),jnp.bfloat16),pltpu.VMEM((2,32,128,128),jnp.bfloat16),D((2,2)),D((2,))]),
      out_shape=jax.ShapeDtypeStruct((128,4,128,128),jnp.bfloat16),
      compiler_params=pltpu.CompilerParams(vmem_limit_bytes=60*2**20),
    )(info,lag,rt,g2,done)


def body(samples, offsets):
    x = spectra(samples, offsets)
    lag = jnp.asarray(lag_np(), dtype=jnp.bfloat16)
    done, g2, rt = main(x, lag)
    band = lax.axis_index("band")
    info = jnp.stack([band * 64, lax.axis_index("wide") * 512, band // 2]).astype(jnp.int32)
    return last(info, lag, rt, g2, done).reshape(2, 64, 512, 128)


def solution(mesh):
    return jax.shard_map(
        body,
        mesh=mesh,
        in_specs=(P(None, "band", "wide"), P("wide")),
        out_specs=P(None, "band", "wide", None),
        check_vma=False,
    )
```

```python
import math

import jax
import jax.numpy as jnp
import ml_dtypes
import numpy as np
from jax import lax
from jax.experimental import pallas as pl
from jax.experimental.pallas import tpu as pltpu
from jax.sharding import PartitionSpec as P

MESH = pl.DeviceIdType.MESH
NQ = 4
NJ = 8
PW = 24
NA = 7
PITCH = 264
FAC = 1 / math.sqrt(32)


def dft_np():
    n=np.arange(512); f=np.arange(256)
    ph=(f[:,None]*n[None,:])%512
    ang=2*np.pi/512*ph
    win=0.5-0.5*np.cos(2*np.pi/512*(n+0.5))
    t=np.concatenate([np.cos(ang)*win, -np.sin(ang)*win],0).astype(ml_dtypes.bfloat16)
    t=t.reshape(2,32,8,512).transpose(1,0,2,3).reshape(512,512).astype(np.float32)
    return np.concatenate([t,np.zeros((512,128),np.float32)],1)

def lag_np():
    f=np.arange(256); l=np.arange(128)-64
    ph=(f[:,None]*l[None,:])%512
    ang=2*np.pi/512*ph
    t=np.concatenate([np.cos(ang)/16,-np.sin(ang)/16],0).astype(ml_dtypes.bfloat16)
    return t.T.copy()

def spec_kernel(off_ref, tab_ref, s_ref, x_ref, tk):
    i=pl.program_id(0)
    @pl.when(i==0)
    def _():
        for k in range(2):
            t=pltpu.roll(tab_ref[...].astype(jnp.float32), off_ref[k]+64*k, 1)
            tk[k]=t.astype(jnp.bfloat16)
    s=s_ref[...].reshape(128,1152)
    a0=lax.dot_general(tk[0], s[:, :640], (((1,),(1,)),((),())), preferred_element_type=jnp.float32)
    a1=lax.dot_general(tk[1], s[:, 512:], (((1,),(1,)),((),())), preferred_element_type=jnp.float32)
    lane=lax.broadcasted_iota(jnp.int32,(512,128),1)<64
    g0=jnp.where(lane,a0,pltpu.roll(a1,64,1))
    g1=jnp.where(lane,pltpu.roll(a0,64,1),a1)
    for j,g in enumerate((g0,g1)):
        v=g.reshape(32,2,8,128)
        re=v[:,0]; im=v[:,1]
        pw=re*re+im*im
        level=jnp.sum(jnp.sum(pw,0),0,keepdims=True)*(0.25/256.0)+1e-6
        inv=lax.rsqrt(pw+level[None])
        x_ref[j]=jnp.stack([re*inv,im*inv],1).reshape(32,16,128).astype(jnp.bfloat16)

def spectra(samples, offsets):
    return pl.pallas_call(spec_kernel,
      grid=(8,),
      in_specs=[pl.BlockSpec(memory_space=pltpu.SMEM), pl.BlockSpec((512,640),lambda i:(0,0)), pl.BlockSpec((2,64,1152),lambda i:(i,0,0))],
      out_specs=pl.BlockSpec((2,32,16,128),lambda i:(i,0,0,0)),
      out_shape=jax.ShapeDtypeStruct((16,32,16,128),jnp.bfloat16),
      scratch_shapes=[pltpu.VMEM((2,512,640),jnp.bfloat16)],
      compiler_params=pltpu.CompilerParams(vmem_limit_bytes=62*2**20),
    )(offsets, jnp.asarray(dft_np(), dtype=jnp.bfloat16), samples)

def relayout_quarter(rcv, tmp, hold, q):
    @pl.loop(0, 8)
    def _(fi):
        fg=q*8+fi
        for xs in range(2):
            for w in range(8):
                tmp[xs, w*PW:w*PW+16, :]=rcv[xs, w, fg].astype(jnp.float32)
        for xs in range(2):
            for f8 in range(8):
                re=tmp[xs, pl.ds(f8,8,stride=PW),:]
                im=tmp[xs, pl.ds(8+f8,8,stride=PW),:]
                hold[xs, fg*8+f8]=jnp.concatenate([re,im],0).astype(jnp.bfloat16)

def join2(a,b):
    return jnp.concatenate([a[:,:64],b[:,:64]],1), jnp.concatenate([a[:,64:],b[:,64:]],1)


def prep_rows(r_ref,fg,tmp,rt):
    for w in range(16):
        y,xs,c=w//4,(w//2)%2,w%2
        for g in range(2):
            tmp[g,xs,(y*2+c)*PW:(y*2+c)*PW+16,:]=r_ref[w,g,fg].astype(jnp.float32)
    for fp in range(4):
        ks=[];ts=[]
        for f8 in (2*fp,2*fp+1):
            parts=[]
            for g in range(2):
                re=[tmp[g,xs,pl.ds(f8,8,stride=PW),:] for xs in range(2)]
                im=[tmp[g,xs,pl.ds(8+f8,8,stride=PW),:] for xs in range(2)]
                parts.append((jnp.concatenate([re[0],im[0],re[1],im[1]],0), jnp.concatenate([im[0],-re[0],im[1],-re[1]],0)))
            ks+=join2(parts[0][0],parts[1][0])
            ts+=join2(parts[0][1],parts[1][1])
        rt[fg*4+fp,0:128]=jnp.concatenate(ks,0).T.astype(jnp.bfloat16)
        rt[fg*4+fp,128:256]=jnp.concatenate(ts,0).T.astype(jnp.bfloat16)


def stage_one(gs,rt,scr,f0,pairs):
    zero=jnp.zeros((64,128),jnp.bfloat16)
    for i in range(pairs):
        parts=[]
        for j in range(2):
            f=f0+2*i+j
            c=jnp.concatenate(join2(gs[0,:,f].reshape(32,128),gs[1,:,f].reshape(32,128)),0)
            parts.append(jnp.concatenate([c,zero] if j==0 else [zero,c],1))
        s=jnp.dot(rt[f0//2+i],jnp.concatenate(parts,0),preferred_element_type=jnp.float32)
        for j in range(2):
            scr[pl.ds(pl.multiple_of((f0+2*i+j)*PITCH,8),256),:]=s[:,j*128:(j+1)*128]


def stage_two(scr,lag,ost,slot_,r0,pairs,row_base,col_base):
    for i in range(pairs):
        rows=[r0+2*i+j for j in range(2)]
        rhs=jnp.concatenate([jnp.concatenate([scr[pl.ds(p*128+r,256,stride=PITCH),:].astype(jnp.bfloat16) for p in range(2)],0) for r in rows],1)
        o=jnp.dot(lag,rhs,preferred_element_type=jnp.float32)
        for j in range(2):
            r=r0+2*i+j
            oc=(o[:,j*128:(j+1)*128]*FAC).T
            row=(r//64)*512+row_base+r%64
            col=col_base+lax.broadcasted_iota(jnp.int32,(128,128),0)
            ost[slot_,2*i+j]=jnp.where(col==row,0.0,oc).astype(jnp.bfloat16)


def main_kernel(x_ref, lag_ref, out_ref, g2_ref, rt_out, r_ref, rcv, tmp, hold, rtmp, rt, gs, scr, ost,
                a_send, a_recv, r_send, r_recv, x_send, zp_send, zm_send, g_recv, l_sem, g_sem, o_sem, t_sem):
    wide=lax.axis_index("wide"); band=lax.axis_index("band")
    y=wide//4; xhi=(wide//2)%2; core=wide%2
    z=band//2; xl=band%2
    zp=(z+1)%4; zm=(z+3)%4; z2=(z+2)%4
    def wid(y_,xh_,c_): return (y_*2+xh_)*2+c_
    def a2a_dev(t):
        dy=t//4; dx=(t//2)%2; dc=t%2
        y_=(y+dy)%4; xh_=(xhi+dx)%2; c_=(core+dc)%2
        return y_,xh_,c_,dx
    dev_x=(wide, z*2+(1-xl)); dev_zp=(wide, zp*2+xl); dev_zm=(wide, zm*2+xl)
    dev_xhi=(wid(y,1-xhi,core), band)
    dev_core=(wid(y,xhi,1-core), band)
    bar=pltpu.get_barrier_semaphore()
    @pl.loop(1,16)
    def _(t):
        y_,xh_,c_,dx=a2a_dev(t)
        pl.semaphore_signal(bar,1,device_id=(wid(y_,xh_,c_), z*2+(xl+dx)%2),device_id_type=MESH)
    for d in (dev_x,dev_zp,dev_zm,dev_xhi):
        pl.semaphore_signal(bar,1,device_id=d,device_id_type=MESH)
    pl.semaphore_wait(bar,19)

    def rc(src,dst,ss,rs,dev):
        return pltpu.make_async_remote_copy(src_ref=src,dst_ref=dst,send_sem=ss,recv_sem=rs,device_id=dev,device_id_type=MESH)

    row_src=x_ref.at[pl.ds(0,2)]
    rows_xhi=rc(row_src, r_ref.at[wide], r_send.at[0], r_recv.at[wide], dev_xhi)
    row_local=pltpu.make_async_copy(row_src, r_ref.at[wide], l_sem.at[0])
    row_local.start()
    own_local=pltpu.make_async_copy(x_ref.at[wide], rcv.at[xhi, y*2+core], l_sem.at[1])
    own_local.start()
    def a2a_copy(t,q):
        y_,xh_,c_,dx=a2a_dev(t)
        fs=pl.ds(q*8,8)
        return rc(x_ref.at[wid(y_,xh_,c_),fs], rcv.at[xhi,y*2+core,fs], a_send.at[t,q], a_recv.at[wide,q],
                  (wid(y_,xh_,c_), z*2+(xl+dx)%2))
    def a2a_wait(t,q):
        dy=t//4; dx=(t//2)%2; dc=t%2
        y_=(y+4-dy)%4; xh_=(xhi+dx)%2; c_=(core+dc)%2
        fs=pl.ds(q*8,8)
        s=wid(y_,xh_,c_)
        rc(x_ref.at[s,fs], rcv.at[xh_,y_*2+c_,fs], a_send.at[t,q], a_recv.at[s,q], dev_x).wait_recv()
    for q in range(2):
        @pl.loop(1,16)
        def _(t):
            a2a_copy(t,q).start()
    def row_y(dy,s,slot):
        return rc(r_ref.at[s], r_ref.at[s], r_send.at[slot], r_recv.at[s], (wid((y+dy)%4,xhi,core),band))
    def row_y_own(dy):
        return rc(row_src, r_ref.at[wide], r_send.at[dy], r_recv.at[wide], (wid((y+dy)%4,xhi,core),band))
    own_core=rc(row_src, r_ref.at[wide], r_send.at[4], r_recv.at[wide], dev_core)

    def slot(zz,xx,cls): return zz*2+(xx+cls)%2, (xhi+cls)%2
    def unit(b,xs,j): return g2_ref.at[b,xs,pl.ds(j*32,32)]
    def send(src,b,xs,j,sems,dev):
        return rc(src, unit(b,xs,j), sems.at[b,xs,j], g_recv.at[b,xs,j], dev)
    def wait_unit(zz,xx,cls,j):
        b,xs=slot(zz,xx,cls)
        send(unit(b,xs,j),b,xs,j,x_send,dev_x).wait_recv()
        return b,xs
    own_local.wait()
    for q in range(NQ):
        @pl.loop(1,16)
        def _(t):
            a2a_wait(t,q)
        relayout_quarter(rcv,tmp,hold,q)
        @pl.loop(q*2,q*2+2)
        def _(j):
            for cls in range(2):
                b,xs=slot(z,xl,cls)
                src=hold.at[xs,pl.ds(j*32,32)]
                send(src,b,xs,j,x_send,dev_x).start()
                send(src,b,xs,j,zp_send,dev_zp).start()
                send(src,b,xs,j,zm_send,dev_zm).start()
                pltpu.make_async_copy(src,unit(b,xs,j),l_sem.at[2+cls*8+j]).start()
        if q+2<NQ:
            @pl.loop(1,16)
            def _(t):
                a2a_copy(t,q+2).start()
        if q==1:
            rows_xhi.start()
        if q==2:
            for dy in (1,3):
                row_y_own(dy).start()
            own_core.start()
    def put(b,xs,j,sems,dev):
        send(unit(b,xs,j),b,xs,j,sems,dev).start()

    def near(j):
        b,xs=wait_unit(z,1-xl,0,j)
        put(b,xs,j,zp_send,dev_zp)
        put(b,xs,j,zm_send,dev_zm)
        b2,xs2=wait_unit(zp,xl,1,j)
        @pl.when(j<NA)
        def _():
            put(b2,xs2,j,x_send,dev_x)
        @pl.when(j>=NA)
        def _():
            b1,xs1=wait_unit(z,1-xl,1,j)
            put(b1,xs1,j,zp_send,dev_zp)
            put(b1,xs1,j,zm_send,dev_zm)

    def row_wait(s):
        rc(row_src,r_ref.at[s],r_send.at[0],r_recv.at[s],dev_x).wait_recv()

    def pass_core(dy,xh_,slot_):
        s=wid((y+dy)%4,xh_,core)
        row_wait(s)
        rc(r_ref.at[s],r_ref.at[s],r_send.at[slot_],r_recv.at[s],dev_core).start()
        return s

    near(0)
    ps=wid(y,1-xhi,core)
    row_wait(ps)
    row_y(1,ps,5).start()
    row_y(3,ps,7).start()
    rc(r_ref.at[ps],r_ref.at[ps],r_send.at[8],r_recv.at[ps],dev_core).start()
    near(1)
    near(2)
    s3=pass_core(3,xhi,10)
    row_y(1,s3,2).start()
    pass_core(1,xhi,9)
    near(3)
    s1=pass_core(1,1-xhi,12)
    row_y(3,s1,6).start()
    pass_core(3,1-xhi,13)
    near(4)
    pass_core(2,xhi,11)
    near(5)
    pass_core(2,1-xhi,14)
    for dy in range(4):
        for xh_ in range(2):
            row_wait(wid((y+dy)%4,xh_,1-core))
    row_local.wait()

    @pl.loop(0,32)
    def _(fg):
        prep_rows(r_ref,fg,rtmp,rt)
        @pl.when(fg%16==7)
        def _():
            near(6+fg//16)
    rt_copy=pltpu.make_async_copy(rt,rt_out,t_sem)
    rt_copy.start()

    def pass_on(j):
        b,xs=wait_unit(zm,xl,1,j)
        @pl.when(j<NA)
        def _():
            put(b,xs,j,x_send,dev_x)
        @pl.when(j%2==0)
        def _():
            put(b,xs,j,zp_send,dev_zp)
        b3,xs3=slot(zp,xl,1)
        @pl.when(j%2==1)
        def _():
            put(b3,xs3,j,zm_send,dev_zm)

    def pass_own(j):
        b1,xs1=wait_unit(zm,xl,0,j)
        b2,xs2=wait_unit(zp,xl,0,j)
        @pl.when(j%2==0)
        def _():
            put(b1,xs1,j,zp_send,dev_zp)
        @pl.when(j%2==1)
        def _():
            put(b2,xs2,j,zm_send,dev_zm)

    def far(j):
        b,xs=wait_unit(z2,xl,1,j)
        @pl.when(j<NA)
        def _():
            put(b,xs,j,x_send,dev_x)

    def across(zz):
        @pl.loop(0,NA)
        def _(j):
            wait_unit(zz,1-xl,1,j)

    def relay():
        @pl.loop(0,NJ)
        def _(j):
            for zz,parity,sems,dev in ((zm,0,zp_send,dev_zp),(zp,1,zm_send,dev_zm)):
                b,xs=wait_unit(zz,1-xl,0,j)
                @pl.when(j%2==parity)
                def _():
                    put(b,xs,j,sems,dev)
                @pl.when(j>=NA)
                def _():
                    b1,xs1=wait_unit(zz,1-xl,1,j)
                    @pl.when(j%2==parity)
                    def _():
                        put(b1,xs1,j,sems,dev)

    @pl.loop(0,NJ)
    def _(j):
        for cls in range(2):
            b,xs=slot(z,xl,cls)
            pltpu.make_async_copy(hold.at[xs,pl.ds(j*32,32)],unit(b,xs,j),l_sem.at[2+cls*8+j]).wait()
    lag=lag_ref[...]
    @pl.loop(0,3)
    def _(s):
        zz=(z+s+s//2)%4
        @pl.when(s==0)
        def _():
            across(z)
        @pl.when(s==1)
        def _():
            relay()
            across(zp)
        @pl.when(s==2)
        def _():
            across(zm)
        def g_copy(j):
            fs=pl.ds(j*32,32)
            return pltpu.make_async_copy(g2_ref.at[pl.ds(zz*2,2),:,fs],gs.at[:,:,fs],g_sem.at[j])
        for j in range(NJ):
            g_copy(j).start()
        @pl.loop(0,NJ)
        def _(j):
            @pl.when(s==0)
            def _():
                pass_on(j)
            g_copy(j).wait()
            stage_one(gs,rt,scr,j*32,16)
        def o_copy(i):
            return pltpu.make_async_copy(ost.at[i%2],out_ref.at[s,pl.ds(i*16,16)],o_sem.at[i%2])
        @pl.loop(0,8)
        def _(i):
            @pl.when(s==0)
            def _():
                pass_own(i)
            @pl.when(s==1)
            def _():
                far(i)
            @pl.when(i>=2)
            def _():
                o_copy(i).wait()
            stage_two(scr,lag,ost,i%2,i*16,8,band*64,wide*512+zz*128)
            o_copy(i).start()
        o_copy(0).wait()
        o_copy(1).wait()

    @pl.loop(0,NJ)
    def _(j):
        wait_unit(z2,xl,0,j)
        wait_unit(z2,1-xl,0,j)
        wait_unit(z2,1-xl,1,j)
    rt_copy.wait()
    for i in range(15):
        rc(row_src,r_ref.at[wide],r_send.at[i],r_recv.at[wide],dev_x).wait_send()
    @pl.loop(1,16)
    def _(t):
        for q in range(NQ):
            a2a_copy(t,q).wait_send()
    def ws(zz,xx,cls,j,sems):
        b,xs=slot(zz,xx,cls)
        send(unit(b,xs,j),b,xs,j,sems,dev_x).wait_send()
    @pl.loop(0,NJ)
    def _(j):
        for cls in range(2):
            b,xs=slot(z,xl,cls)
            ws(z,xl,cls,j,x_send)
            ws(z,xl,cls,j,zp_send); ws(z,xl,cls,j,zm_send)
        ws(z,1-xl,0,j,zp_send); ws(z,1-xl,0,j,zm_send)
        @pl.when(j>=NA)
        def _():
            ws(z,1-xl,1,j,zp_send); ws(z,1-xl,1,j,zm_send)
        @pl.when(j<NA)
        def _():
            for zz in (zm,zp,z2): ws(zz,xl,1,j,x_send)
        for zz,parity,sems in ((zm,0,zp_send),(zp,1,zm_send)):
            @pl.when(j%2==parity)
            def _():
                ws(zz,xl,0,j,sems); ws(zz,xl,1,j,sems); ws(zz,1-xl,0,j,sems)
                @pl.when(j>=NA)
                def _():
                    ws(zz,1-xl,1,j,sems)


def main(x,lag):
    D=pltpu.SemaphoreType.DMA
    A=pl.BlockSpec(memory_space=pl.ANY)
    bf=jnp.bfloat16
    return pl.pallas_call(main_kernel,
      in_specs=[A,pl.BlockSpec(memory_space=pltpu.VMEM)],
      out_specs=[A]*3,
      out_shape=[jax.ShapeDtypeStruct((3,128,128,128),bf),jax.ShapeDtypeStruct((8,2,256,16,128),bf),jax.ShapeDtypeStruct((128,256,128),bf)],
      scratch_shapes=[pltpu.VMEM((16,2,32,16,128),bf),pltpu.VMEM((2,8,32,16,128),bf),pltpu.VMEM((2,8*PW,128),jnp.float32),pltpu.VMEM((2,256,16,128),bf),
        pltpu.VMEM((2,2,8*PW,128),jnp.float32),pltpu.VMEM((128,256,128),bf),
        pltpu.VMEM((2,2,256,16,128),bf),pltpu.VMEM((256*PITCH,128),jnp.float32),pltpu.VMEM((2,16,128,128),bf),
        D((16,4)),D((16,4)),D((16,)),D((16,)),D((8,2,8)),D((8,2,8)),D((8,2,8)),D((8,2,8)),D((18,)),D((8,)),D((2,)),D(())],
      compiler_params=pltpu.CompilerParams(collective_id=0,has_side_effects=True,vmem_limit_bytes=60*2**20),
    )(x,lag)


def last_kernel(info_ref,lag_ref,rt_ref,g_ref,done_ref,out_ref,scr,ost,buf,c_sem,o_sem):
    t=pl.program_id(0)
    z=info_ref[2]
    far=(z+2)%4
    def takes(c):
        return [pltpu.make_async_copy(done_ref.at[c//4,pl.ds((c%4)*32+8*h,8)],buf.at[c%3,pl.ds(8*h,8)],c_sem.at[0,c%3,h]) for h in range(4)]
    def gives(c):
        s=c//4
        return [pltpu.make_async_copy(buf.at[c%3,pl.ds(8*h,8)],out_ref.at[pl.ds((c%4)*32+8*h,8),(z+s+s//2)%4],c_sem.at[1,c%3,h]) for h in range(4)]
    @pl.when(t==0)
    def _():
        for d in takes(0)+takes(1):
            d.start()
    for d in takes(t):
        d.wait()
    for d in gives(t):
        d.start()
    @pl.when(t>=1)
    def _():
        for d in gives(t-1):
            d.wait()
    @pl.when(t<10)
    def _():
        for d in takes(t+2):
            d.start()
    @pl.when(t<4)
    def _():
        @pl.loop(0,2)
        def _(i0):
            for i in range(16):
                parts=[]
                zero=jnp.zeros((64,128),jnp.bfloat16)
                for j in range(2):
                    f=i0*32+2*i+j
                    c=jnp.concatenate(join2(g_ref[0,:,f].reshape(32,128),g_ref[1,:,f].reshape(32,128)),0)
                    parts.append(jnp.concatenate([c,zero] if j==0 else [zero,c],1))
                s=jnp.dot(rt_ref[i0*16+i],jnp.concatenate(parts,0),preferred_element_type=jnp.float32)
                for j in range(2):
                    scr[pl.ds(pl.multiple_of((t*64+i0*32+2*i+j)*PITCH,8),256),:]=s[:,j*128:(j+1)*128]
    @pl.when(t>=4)
    def _():
        i=t-4
        def o_copy(i):
            return pltpu.make_async_copy(ost.at[i%2],out_ref.at[pl.ds(i*16,16),far],o_sem.at[i%2])
        @pl.when(i>=2)
        def _():
            o_copy(i).wait()
        stage_two(scr,lag_ref[...],ost,i%2,i*16,8,info_ref[0],info_ref[1]+far*128)
        o_copy(i).start()
        @pl.when(i==7)
        def _():
            o_copy(0).wait()
            o_copy(1).wait()
            for d in gives(11):
                d.wait()


def last(info,lag,rt,g2,done):
    D=pltpu.SemaphoreType.DMA
    A=pl.BlockSpec(memory_space=pl.ANY)
    q=lambda t: jnp.minimum(t,3)
    return pl.pallas_call(last_kernel,
      grid_spec=pltpu.PrefetchScalarGridSpec(num_scalar_prefetch=1,grid=(12,),
        in_specs=[pl.BlockSpec((128,512),lambda t,i:(0,0)),
          pl.BlockSpec((32,256,128),lambda t,i:(q(t),0,0)),
          pl.BlockSpec((2,2,64,16,128),lambda t,i:((i[2]+2)%4,0,q(t),0,0)),A],
        out_specs=A,
        scratch_shapes=[pltpu.VMEM((256*PITCH,128),jnp.float32),pltpu.VMEM((2,16,128,128),jnp.bfloat16),pltpu.VMEM((3,32,128,128),jnp.bfloat16),D((2,3,4)),D((2,))]),
      out_shape=jax.ShapeDtypeStruct((128,4,128,128),jnp.bfloat16),
      compiler_params=pltpu.CompilerParams(vmem_limit_bytes=60*2**20),
    )(info,lag,rt,g2,done)


def body(samples, offsets):
    x = spectra(samples, offsets)
    lag = jnp.asarray(lag_np(), dtype=jnp.bfloat16)
    done, g2, rt = main(x, lag)
    band = lax.axis_index("band")
    info = jnp.stack([band * 64, lax.axis_index("wide") * 512, band // 2]).astype(jnp.int32)
    return last(info, lag, rt, g2, done).reshape(2, 64, 512, 128)


def solution(mesh):
    return jax.shard_map(
        body,
        mesh=mesh,
        in_specs=(P(None, "band", "wide"), P("wide")),
        out_specs=P(None, "band", "wide", None),
        check_vma=False,
    )
```
